32 devices in a mesh: slab: 8 (over z, x), elec: 4 (over y, core).
Axes of the slice: x: 2, y: 2, z: 4, core: 2. Of those that a mesh axis runs over, the one named last changes fastest.
Arguments:
- potentials: float32 [128, 16, 128, 128], P('elec', None, 'slab'), may hold values from -6 to 6
- conductivity: float32 [16, 128, 128], P(None, 'slab'), may hold values from 0.1 to 1
- quadrupoles: int32 [512, 4], P('elec'), may hold values from 0 to 127, as said below
Outputs:
- jacobian: bfloat16 [512, 16, 128, 128], P('elec', 'slab')
The draws below stay inside these ranges and needn't reach their ends.
Inputs may be any that keep to these rules, and one draw needn't show every extreme that they name: `quadrupoles`: rows g * 128 to (g + 1) * 128 - 1 are the measurements of group g; electrode e belongs to group e // 32. A and B are two different electrodes of the row's own group; M and N are two different electrodes of other groups. The rows of one group name, in M or N, at most 4 different electrodes of any one other group, and exactly 4 of some other group.
All inputs are finite; a program needn't handle non-finite values.
Results may differ from the reference program's by a relative error of at most 0.0058.
Values may be sent and summed in bfloat16 or wider, within the bound.
A program may use at most 256 MiB of HBM per device.

```python
import math
import jax
import jax.numpy as jnp
from jax import lax

CELLS_ALONG_X = 128
CELLS_ALONG_Y = 128
GROUP_CURRENTS = 32
GROUP_READINGS = 128
REQ = 4
CELLS_ALONG_Z = 16
E = 128
TOTAL_READINGS = 512
N_ELEC = 4


def draw_quadrupoles(key, part):
    block_list = []
    for group_idx in range(N_ELEC):
        group_key = jax.random.fold_in(key, group_idx)
        key_sequence = jax.random.split(group_key, 4 + N_ELEC)
        first_local_index = jax.random.randint(key_sequence[0], (GROUP_READINGS,), 0, GROUP_CURRENTS)
        second_local_index = (first_local_index + jax.random.randint(key_sequence[1], (GROUP_READINGS,), 1, GROUP_CURRENTS)) % GROUP_CURRENTS
        member_list = []
        valid_list = []
        for offset in range(1, N_ELEC):
            other_group = (group_idx + offset) % N_ELEC
            chosen = jax.random.permutation(key_sequence[3 + offset], GROUP_CURRENTS)[:REQ] + other_group * GROUP_CURRENTS
            if offset == 1:
                limit = REQ
            else:
                limit = jax.random.randint(jax.random.fold_in(key_sequence[2], offset), (), 1, REQ + 1)
            member_list.append(chosen)
            valid_list.append(jnp.arange(REQ) < limit)
        members = jnp.concatenate(member_list, 0)
        valid_flags = jnp.concatenate(valid_list, 0)
        ranking = jnp.where(valid_flags, 0, members.shape[0]) + jnp.arange(members.shape[0])
        eligible = members[jnp.argsort(ranking)]
        length_total = jnp.sum(valid_flags.astype(jnp.int32))
        row_index_list = jnp.arange(GROUP_READINGS)
        probe_first = eligible[row_index_list % length_total]
        shift_amount = jax.random.randint(key_sequence[3], (GROUP_READINGS,), 0, length_total - 1)
        probe_second = eligible[(row_index_list + 1 + shift_amount) % length_total]
        block_list.append(jnp.stack([group_idx * GROUP_CURRENTS + first_local_index, group_idx * GROUP_CURRENTS + second_local_index, probe_first, probe_second], 1))
    return jnp.concatenate(block_list, 0).astype(jnp.int32)


def level_of(key, shape, cuts, low, top_value):
    gain, own = 1.0, jax.random.fold_in(key, 6)
    for dim, shards_of in cuts:
        steps = jnp.exp(jax.random.uniform(jax.random.fold_in(own, dim), (shards_of,), jnp.float32, low / len(cuts), top_value / len(cuts)))
        gain = gain * jnp.repeat(steps, shape[dim] // shards_of).reshape([-1 if axis == dim else 1 for axis in range(len(shape))])
    return gain


def bell_draw(own_key, extent, scale, most, pieces=(), kind=jnp.bfloat16):
    result = scale * jax.random.normal(own_key, extent, jnp.float32)
    if pieces:
        result = result * level_of(own_key, extent, pieces, -0.22, 0.18)
    return jnp.clip(result, -most, most).astype(kind)


def setup_inputs(seed: int = 0) -> dict:
    keys = jax.random.split(jax.random.key(seed), 4)
    return {
        "potentials": bell_draw(keys[0], (E, CELLS_ALONG_Z, CELLS_ALONG_X, CELLS_ALONG_Y), 1.0, 6.0, ((0, 4), (2, 8)), jnp.float32),
        "conductivity": jnp.clip(jnp.exp(math.log(1.0) - 2.3025851 * jax.random.uniform(keys[1], (CELLS_ALONG_Z, CELLS_ALONG_X, CELLS_ALONG_Y), jnp.float32) ** level_of(keys[1], (CELLS_ALONG_Z, CELLS_ALONG_X, CELLS_ALONG_Y), ((1, 8),), -0.2, 0.2)), 0.1, 1.0),
        "quadrupoles": draw_quadrupoles(jax.random.fold_in(keys[3], 71), 0),
    }


def gradients(potentials):
    padded = jnp.pad(potentials, ((0, 0), (1, 1), (1, 1), (1, 1)))
    grad_z = (padded[:, 2:, 1:-1, 1:-1] - padded[:, :-2, 1:-1, 1:-1]) * 0.5
    grad_x = (padded[:, 1:-1, 2:, 1:-1] - padded[:, 1:-1, :-2, 1:-1]) * 0.5
    grad_y = (padded[:, 1:-1, 1:-1, 2:] - padded[:, 1:-1, 1:-1, :-2]) * 0.5
    return jnp.stack([grad_z, grad_x, grad_y], 1).astype(jnp.bfloat16)


def reference(potentials, conductivity, quadrupoles):
    grad = gradients(potentials)

    def block_rows(quad_block):
        source_grad = grad[quad_block[:, 0]].astype(jnp.float32) - grad[quad_block[:, 1]].astype(jnp.float32)
        probe_grad = grad[quad_block[:, 2]].astype(jnp.float32) - grad[quad_block[:, 3]].astype(jnp.float32)
        summed = jnp.sum(source_grad * probe_grad, axis=1)
        return (-(conductivity[None] * summed)).astype(jnp.bfloat16)

    number_of_blocks = TOTAL_READINGS // 16
    output_rows = lax.map(block_rows, quadrupoles.reshape(number_of_blocks, 16, 4))
    return output_rows.reshape(TOTAL_READINGS, CELLS_ALONG_Z, CELLS_ALONG_X, CELLS_ALONG_Y)
```

```python
import functools

import jax
import jax.numpy as jnp
from jax import lax
from jax.experimental import pallas as pl
from jax.experimental.pallas import tpu as pltpu
from jax.sharding import PartitionSpec as P

MESH = pl.DeviceIdType.MESH
REQ = 4


def lists(quadrupoles, per_group, groups):
    me = lax.axis_index("elec")
    ids = jnp.arange(per_group * groups, dtype=jnp.int32)
    owner = ids // per_group
    away = (owner - me) % groups
    named = jnp.any(quadrupoles[:, 2:4].reshape(-1)[:, None] == ids[None, :], axis=0)
    before = (owner[:, None] == owner[None, :]) & (ids[None, :] < ids[:, None])
    rank = jnp.sum((before & named[None, :]).astype(jnp.int32), axis=1)
    other = per_group + (away - 1) * REQ + jnp.minimum(rank, REQ - 1)
    slot = jnp.where(away == 0, ids - me * per_group, other)
    index = jnp.sum(jnp.where(quadrupoles[:, :, None] == ids, slot, 0), axis=-1)
    steps = jnp.arange(groups, dtype=jnp.int32)[:, None, None]
    lanes = jnp.arange(128, dtype=jnp.int32)[None, :, None]
    hit = named & (away == steps) & (rank == lanes)
    asked = jnp.sum(jnp.where(hit, ids % per_group, 0), axis=-1)
    return index.astype(jnp.int32), jnp.broadcast_to(asked[:, None, :], (groups, 8, 128))


def exchange_kernel(slabs, groups, planes, *refs):
    pot, cond, asked, table_out, weight_out = refs[:5]
    pot_v, gz_src, asked_in, asked_s, weight_v = refs[5:10]
    p_in = refs[10 : 10 + planes]
    own = refs[10 + planes : 10 + 2 * planes]
    far = refs[10 + 2 * planes : 10 + 3 * planes]
    out_box = refs[10 + 3 * planes : 10 + 4 * planes]
    (slab_send, slab_recv, cond_send, cond_recv, ask_send, ask_recv, far_send, far_recv, local) = refs[10 + 4 * planes :]

    count, depth, rows, width = pot.shape
    me = lax.axis_index("slab")
    group = lax.axis_index("elec")
    my_rows = pl.ds(pl.multiple_of(me * rows, rows), rows)

    stage = pltpu.make_async_copy(pot, pot_v, local.at[0])
    stage.start()

    barrier = pltpu.get_barrier_semaphore()
    for step in range(1, slabs):
        pl.semaphore_signal(barrier, inc=1, device_id={"slab": lax.rem(me + step, slabs)}, device_id_type=MESH)
    for step in range(1, groups):
        pl.semaphore_signal(barrier, inc=1, device_id={"elec": lax.rem(group + step, groups)}, device_id_type=MESH)
    pl.semaphore_wait(barrier, slabs + groups - 2)

    asks = []
    for step in range(1, groups):
        copy = pltpu.make_async_remote_copy(
            src_ref=asked.at[step],
            dst_ref=asked_in.at[step],
            send_sem=ask_send.at[step],
            recv_sem=ask_recv.at[step],
            device_id={"elec": lax.rem(group + step, groups)},
            device_id_type=MESH,
        )
        copy.start()
        asks.append(copy)

    def p_copy(plane, step):
        to = lax.rem(me + step, slabs)
        return pltpu.make_async_remote_copy(
            src_ref=pot.at[:, to * planes + plane],
            dst_ref=p_in[plane].at[:, my_rows, :],
            send_sem=slab_send.at[0, plane, step],
            recv_sem=slab_recv.at[0, plane, step],
            device_id={"slab": to},
            device_id_type=MESH,
        )

    def gz_copy(plane, step):
        to = lax.rem(me + step, slabs)
        return pltpu.make_async_remote_copy(
            src_ref=gz_src.at[plane, to],
            dst_ref=own[plane].at[:, 0, my_rows, :],
            send_sem=slab_send.at[1, plane, step],
            recv_sem=slab_recv.at[1, plane, step],
            device_id={"slab": to},
            device_id_type=MESH,
        )

    def cond_copy(step):
        to = lax.rem(me + step, slabs)
        return pltpu.make_async_remote_copy(
            src_ref=cond.at[pl.ds(to * planes, planes)],
            dst_ref=weight_v.at[:, my_rows, :],
            send_sem=cond_send.at[step],
            recv_sem=cond_recv.at[step],
            device_id={"slab": to},
            device_id_type=MESH,
        )

    def p_local(plane):
        return pltpu.make_async_copy(pot.at[:, me * planes + plane], p_in[plane].at[:, my_rows, :], local.at[1 + plane])

    def gz_local(plane):
        return pltpu.make_async_copy(
            gz_src.at[plane, me], own[plane].at[:, 0, my_rows, :], local.at[1 + planes + plane]
        )

    cond_local = pltpu.make_async_copy(
        cond.at[pl.ds(me * planes, planes)], weight_v.at[:, my_rows, :], local.at[1 + 2 * planes]
    )

    for plane in range(planes):
        for step in range(1, slabs):
            p_copy(plane, step).start()
        p_local(plane).start()
        if plane == 0:
            stage.wait()

        @pl.loop(0, count)
        def _(e, plane=plane):
            for to in range(slabs):
                z = to * planes + plane
                above = pot_v[e, z + 1] if z + 1 < depth else jnp.zeros((rows, width), jnp.float32)
                below = pot_v[e, z - 1] if z > 0 else jnp.zeros((rows, width), jnp.float32)
                gz_src[plane, to, e] = ((above - below) * 0.5).astype(jnp.bfloat16)

        for step in range(1, slabs):
            gz_copy(plane, step).start()
        gz_local(plane).start()
    for step in range(1, slabs):
        cond_copy(step).start()
    cond_local.start()

    for copy in asks:
        copy.wait()
    to_scalar = pltpu.make_async_copy(asked_in, asked_s, local.at[2 + 2 * planes])
    to_scalar.start()
    to_scalar.wait()

    x_size = p_in[0].shape[1]
    row = lax.broadcasted_iota(jnp.int32, (x_size, width), 0)
    lane = lax.broadcasted_iota(jnp.int32, (x_size, width), 1)

    def far_copy(plane, step):
        return pltpu.make_async_remote_copy(
            src_ref=out_box[plane].at[step - 1],
            dst_ref=far[plane].at[groups - 1 - step],
            send_sem=far_send.at[plane, step],
            recv_sem=far_recv.at[plane, step],
            device_id={"elec": lax.rem(group + step, groups)},
            device_id_type=MESH,
        )

    def own_out(plane):
        return pltpu.make_async_copy(
            own[plane], table_out.at[plane, pl.ds(0, count)], local.at[3 + 2 * planes + plane]
        )

    def far_out(plane, place):
        return pltpu.make_async_copy(
            far[plane].at[place],
            table_out.at[plane, pl.ds(count + place * REQ, REQ)],
            local.at[3 + 3 * planes + plane * (groups - 1) + place],
        )

    for plane in range(planes):
        for step in range(1, slabs):
            p_copy(plane, step).wait_recv()
            gz_copy(plane, step).wait_recv()
        p_local(plane).wait()
        gz_local(plane).wait()

        @pl.loop(0, count)
        def _(e, plane=plane):
            p = p_in[plane][e]
            up = jnp.where(row < x_size - 1, pltpu.roll(p, x_size - 1, 0), 0.0)
            down = jnp.where(row > 0, pltpu.roll(p, 1, 0), 0.0)
            own[plane][e, 1] = ((up - down) * 0.5).astype(jnp.bfloat16)
            right = jnp.where(lane < width - 1, pltpu.roll(p, width - 1, 1), 0.0)
            left = jnp.where(lane > 0, pltpu.roll(p, 1, 1), 0.0)
            own[plane][e, 2] = ((right - left) * 0.5).astype(jnp.bfloat16)

        for step in range(1, groups):
            for place in range(REQ):
                chosen = asked_s[groups - step, 0, place]
                for d in range(3):
                    out_box[plane][step - 1, place, d] = own[plane][chosen, d]
            far_copy(plane, step).start()
        own_out(plane).start()

    for step in range(1, slabs):
        cond_copy(step).wait_recv()
    cond_local.wait()
    weight_done = pltpu.make_async_copy(weight_v, weight_out, local.at[2 + 2 * planes])
    weight_done.start()
    for plane in range(planes):
        for step in range(1, groups):
            far_copy(plane, step).wait_recv()
            far_out(plane, groups - 1 - step).start()
    for plane in range(planes):
        own_out(plane).wait()
        for place in range(groups - 1):
            far_out(plane, place).wait()
        for step in range(1, groups):
            far_copy(plane, step).wait_send()
        for step in range(1, slabs):
            p_copy(plane, step).wait_send()
            gz_copy(plane, step).wait_send()
    for step in range(1, slabs):
        cond_copy(step).wait_send()
    weight_done.wait()


def exchange(potentials, conductivity, asked, slabs, groups):
    count, depth, rows, width = potentials.shape
    planes = depth // slabs
    x_size = rows * slabs
    table_rows = count + (groups - 1) * REQ
    hbm = pl.BlockSpec(memory_space=pl.ANY)
    dma = pltpu.SemaphoreType.DMA
    bf16, f32 = jnp.bfloat16, jnp.float32
    return pl.pallas_call(
        functools.partial(exchange_kernel, slabs, groups, planes),
        out_shape=[
            jax.ShapeDtypeStruct((planes, table_rows, 3, x_size, width), bf16),
            jax.ShapeDtypeStruct((planes, x_size, width), f32),
        ],
        in_specs=[hbm, hbm, pl.BlockSpec(memory_space=pltpu.VMEM)],
        out_specs=[hbm, hbm],
        scratch_shapes=[
            pltpu.VMEM((count, depth, rows, width), f32),
            pltpu.VMEM((planes, slabs, count, rows, width), bf16),
            pltpu.VMEM((groups, 8, 128), jnp.int32),
            pltpu.SMEM((groups, 8, 128), jnp.int32),
            pltpu.VMEM((planes, x_size, width), f32),
        ]
        + [pltpu.VMEM((count, x_size, width), f32)] * planes
        + [pltpu.VMEM((count, 3, x_size, width), bf16)] * planes
        + [pltpu.VMEM((groups - 1, REQ, 3, x_size, width), bf16)] * planes
        + [pltpu.VMEM((groups - 1, REQ, 3, x_size, width), bf16)] * planes
        + [
            dma((2, planes, slabs)),
            dma((2, planes, slabs)),
            dma((slabs,)),
            dma((slabs,)),
            dma((groups,)),
            dma((groups,)),
            dma((planes, groups)),
            dma((planes, groups)),
            dma((3 + 3 * planes + planes * (groups - 1),)),
        ],
        compiler_params=pltpu.CompilerParams(
            collective_id=0, has_side_effects=True, vmem_limit_bytes=48 * 1024 * 1024
        ),
        name="exchange",
    )(potentials, conductivity, asked)


def rows_kernel(index, table, weight, out):
    w = -weight[0]
    readings = out.shape[0]

    def reading(m):
        a, b, c, d = index[4 * m], index[4 * m + 1], index[4 * m + 2], index[4 * m + 3]
        total = None
        for way in range(3):
            source = table[0, a, way].astype(jnp.float32) - table[0, b, way].astype(jnp.float32)
            probe = table[0, c, way].astype(jnp.float32) - table[0, d, way].astype(jnp.float32)
            term = source * probe
            total = term if total is None else total + term
        out[m, 0] = (w * total).astype(jnp.bfloat16)

    @pl.loop(0, readings // 4)
    def _(block):
        for k in range(4):
            reading(block * 4 + k)


def jacobian_rows(index, table, weight):
    planes, table_rows, ways, x_size, width = table.shape
    readings = index.shape[0]
    part = 32
    return pl.pallas_call(
        rows_kernel,
        out_shape=jax.ShapeDtypeStruct((readings, planes, x_size, width), jnp.bfloat16),
        grid_spec=pltpu.PrefetchScalarGridSpec(
            num_scalar_prefetch=1,
            grid=(planes, x_size // part),
            in_specs=[
                pl.BlockSpec((1, table_rows, ways, part, width), lambda z, x, _: (z, 0, 0, x, 0)),
                pl.BlockSpec((1, part, width), lambda z, x, _: (z, x, 0)),
            ],
            out_specs=pl.BlockSpec((readings, 1, part, width), lambda z, x, _: (0, z, x, 0)),
        ),
        compiler_params=pltpu.CompilerParams(vmem_limit_bytes=32 * 1024 * 1024),
        name="rows",
    )(index.reshape(-1), table, weight)


def general(potentials, conductivity, quadrupoles):
    shifted = lax.all_to_all(potentials, "slab", split_axis=1, concat_axis=2, tiled=True)
    cond = lax.all_to_all(conductivity[None], "slab", split_axis=1, concat_axis=2, tiled=True)[0]
    slabs = lax.axis_size("slab")
    ends = slabs - 1
    last = shifted.shape[1] - 1
    below = lax.ppermute(shifted[:, last:], "slab", [(i, i + 1) for i in range(ends)])
    above = lax.ppermute(shifted[:, :1], "slab", [(i + 1, i) for i in range(ends)])
    tall = jnp.concatenate([below, shifted, above], axis=1)
    wide = jnp.pad(shifted, ((0, 0), (0, 0), (1, 1), (1, 1)))
    grads = jnp.stack(
        [
            (tall[:, 2:] - tall[:, :-2]) * 0.5,
            (wide[:, :, 2:, 1:-1] - wide[:, :, :-2, 1:-1]) * 0.5,
            (wide[:, :, 1:-1, 2:] - wide[:, :, 1:-1, :-2]) * 0.5,
        ],
        1,
    ).astype(jnp.bfloat16)
    table = lax.all_gather(grads.reshape(grads.shape[0], 3, -1), "elec", axis=0, tiled=True)
    ids = jnp.arange(table.shape[0], dtype=jnp.int32)
    hot = (quadrupoles[:, :, None] == ids).astype(jnp.bfloat16)
    flat = table.reshape(table.shape[0], -1)
    shape = (quadrupoles.shape[0], 3, -1)
    source = jnp.dot(hot[:, 0] - hot[:, 1], flat, preferred_element_type=jnp.float32).reshape(shape)
    probe = jnp.dot(hot[:, 2] - hot[:, 3], flat, preferred_element_type=jnp.float32).reshape(shape)
    rows = -(cond.reshape(-1)[None] * jnp.sum(source * probe, axis=1))
    return rows.astype(jnp.bfloat16).reshape((quadrupoles.shape[0],) + shifted.shape[1:])


def shards(potentials, conductivity, quadrupoles):
    slabs, groups = lax.axis_size("slab"), lax.axis_size("elec")
    count, depth, rows, width = potentials.shape
    if rows % 16 or width % 128 or depth % slabs or (rows * slabs) % 32 or quadrupoles.shape[0] % 4:
        return general(potentials, conductivity, quadrupoles)
    index, asked = lists(quadrupoles, count, groups)
    table, weight = exchange(potentials, conductivity, asked, slabs, groups)
    return jacobian_rows(index, table, weight)


def solution(mesh):
    in_specs = (P("elec", None, "slab", None), P(None, "slab", None), P("elec", None))
    out_specs = P("elec", "slab", None, None)
    return jax.shard_map(shards, mesh=mesh, in_specs=in_specs, out_specs=out_specs, check_vma=False)
```

```python
import functools

import jax
import jax.numpy as jnp
from jax import lax
from jax.experimental import pallas as pl
from jax.experimental.pallas import tpu as pltpu
from jax.sharding import PartitionSpec as P

MESH = pl.DeviceIdType.MESH
REQ = 4
PARTS = 4


def lists(quadrupoles, per_group, groups):
    me = lax.axis_index("elec")
    ids = jnp.arange(per_group * groups, dtype=jnp.int32)
    owner = ids // per_group
    away = (owner - me) % groups
    named = jnp.any(quadrupoles[:, 2:4].reshape(-1)[:, None] == ids[None, :], axis=0)
    before = (owner[:, None] == owner[None, :]) & (ids[None, :] < ids[:, None])
    rank = jnp.sum((before & named[None, :]).astype(jnp.int32), axis=1)
    other = (away - 1) * REQ + jnp.minimum(rank, REQ - 1)
    slot = jnp.where(away == 0, ids - me * per_group, other)
    index = jnp.sum(jnp.where(quadrupoles[:, :, None] == ids, slot, 0), axis=-1)
    steps = jnp.arange(groups, dtype=jnp.int32)[:, None, None]
    lanes = jnp.arange(128, dtype=jnp.int32)[None, :, None]
    hit = named & (away == steps) & (rank == lanes)
    asked = jnp.sum(jnp.where(hit, ids % per_group, 0), axis=-1)
    return index.astype(jnp.int32), jnp.broadcast_to(asked[:, None, :], (groups, 8, 128))


def exchange_kernel(slabs, groups, planes, *refs):
    pot, cond, asked, index, out = refs[:5]
    pot_v, gz_src, asked_in, asked_s, weight_v = refs[5:10]
    p_in = refs[10 : 10 + planes]
    own = refs[10 + planes : 10 + 2 * planes]
    stop = 10 + 2 * planes + planes * PARTS
    far = refs[10 + 2 * planes : stop]
    out_box = refs[stop : stop + planes * PARTS]
    result = refs[stop + planes * PARTS : stop + planes * PARTS + 2]
    (slab_send, slab_recv, cond_send, cond_recv, ask_send, ask_recv, far_send, far_recv, local) = refs[
        stop + planes * PARTS + 2 :
    ]

    count, depth, rows, width = pot.shape
    me = lax.axis_index("slab")
    group = lax.axis_index("elec")
    my_rows = pl.ds(pl.multiple_of(me * rows, rows), rows)

    stage = pltpu.make_async_copy(pot, pot_v, local.at[0])
    stage.start()

    barrier = pltpu.get_barrier_semaphore()
    for step in range(1, slabs):
        pl.semaphore_signal(barrier, inc=1, device_id={"slab": lax.rem(me + step, slabs)}, device_id_type=MESH)
    for step in range(1, groups):
        pl.semaphore_signal(barrier, inc=1, device_id={"elec": lax.rem(group + step, groups)}, device_id_type=MESH)
    pl.semaphore_wait(barrier, slabs + groups - 2)

    asks = []
    for step in range(1, groups):
        copy = pltpu.make_async_remote_copy(
            src_ref=asked.at[step],
            dst_ref=asked_in.at[step],
            send_sem=ask_send.at[step],
            recv_sem=ask_recv.at[step],
            device_id={"elec": lax.rem(group + step, groups)},
            device_id_type=MESH,
        )
        copy.start()
        asks.append(copy)

    def p_copy(plane, step):
        to = lax.rem(me + step, slabs)
        return pltpu.make_async_remote_copy(
            src_ref=pot.at[:, to * planes + plane],
            dst_ref=p_in[plane].at[:, my_rows, :],
            send_sem=slab_send.at[0, plane, step],
            recv_sem=slab_recv.at[0, plane, step],
            device_id={"slab": to},
            device_id_type=MESH,
        )

    def gz_copy(plane, step):
        to = lax.rem(me + step, slabs)
        return pltpu.make_async_remote_copy(
            src_ref=gz_src.at[plane, to],
            dst_ref=own[plane].at[:, 0, my_rows, :],
            send_sem=slab_send.at[1, plane, step],
            recv_sem=slab_recv.at[1, plane, step],
            device_id={"slab": to},
            device_id_type=MESH,
        )

    def cond_copy(step):
        to = lax.rem(me + step, slabs)
        return pltpu.make_async_remote_copy(
            src_ref=cond.at[pl.ds(to * planes, planes)],
            dst_ref=weight_v.at[:, my_rows, :],
            send_sem=cond_send.at[step],
            recv_sem=cond_recv.at[step],
            device_id={"slab": to},
            device_id_type=MESH,
        )

    def p_local(plane):
        return pltpu.make_async_copy(pot.at[:, me * planes + plane], p_in[plane].at[:, my_rows, :], local.at[1 + plane])

    def gz_local(plane):
        return pltpu.make_async_copy(
            gz_src.at[plane, me], own[plane].at[:, 0, my_rows, :], local.at[1 + planes + plane]
        )

    cond_local = pltpu.make_async_copy(
        cond.at[pl.ds(me * planes, planes)], weight_v.at[:, my_rows, :], local.at[1 + 2 * planes]
    )

    for step in range(1, slabs):
        cond_copy(step).start()
    cond_local.start()
    for plane in range(planes):
        for step in range(1, slabs):
            p_copy(plane, step).start()
        p_local(plane).start()
        if plane == 0:
            stage.wait()

        @pl.loop(0, count)
        def _(e, plane=plane):
            for to in range(slabs):
                z = to * planes + plane
                above = pot_v[e, z + 1] if z + 1 < depth else jnp.zeros((rows, width), jnp.float32)
                below = pot_v[e, z - 1] if z > 0 else jnp.zeros((rows, width), jnp.float32)
                gz_src[plane, to, e] = ((above - below) * 0.5).astype(jnp.bfloat16)

        for step in range(1, slabs):
            gz_copy(plane, step).start()
        gz_local(plane).start()
    for copy in asks:
        copy.wait()
    to_scalar = pltpu.make_async_copy(asked_in, asked_s, local.at[2 + 2 * planes])
    to_scalar.start()
    to_scalar.wait()

    for step in range(1, slabs):
        cond_copy(step).wait_recv()
    cond_local.wait()

    x_size = p_in[0].shape[1]
    part = x_size // PARTS
    readings = out.shape[0]
    row = lax.broadcasted_iota(jnp.int32, (x_size, width), 0)
    lane = lax.broadcasted_iota(jnp.int32, (x_size, width), 1)

    def far_copy(chunk, step):
        return pltpu.make_async_remote_copy(
            src_ref=out_box[chunk].at[step - 1],
            dst_ref=far[chunk].at[pl.ds((groups - 1 - step) * REQ, REQ)],
            send_sem=far_send.at[chunk, step],
            recv_sem=far_recv.at[chunk, step],
            device_id={"elec": lax.rem(group + step, groups)},
            device_id_type=MESH,
        )

    def result_copy(chunk):
        plane, place = divmod(chunk, PARTS)
        return pltpu.make_async_copy(
            result[chunk % 2], out.at[:, plane, pl.ds(place * part, part), :], local.at[3 + 2 * planes + chunk % 2]
        )

    for plane in range(planes):
        for step in range(1, slabs):
            p_copy(plane, step).wait_recv()
            gz_copy(plane, step).wait_recv()
        p_local(plane).wait()
        gz_local(plane).wait()

        @pl.loop(0, count)
        def _(e, plane=plane):
            p = p_in[plane][e]
            up = jnp.where(row < x_size - 1, pltpu.roll(p, x_size - 1, 0), 0.0)
            down = jnp.where(row > 0, pltpu.roll(p, 1, 0), 0.0)
            own[plane][e, 1] = ((up - down) * 0.5).astype(jnp.bfloat16)
            right = jnp.where(lane < width - 1, pltpu.roll(p, width - 1, 1), 0.0)
            left = jnp.where(lane > 0, pltpu.roll(p, 1, 1), 0.0)
            own[plane][e, 2] = ((right - left) * 0.5).astype(jnp.bfloat16)

        for place in range(PARTS):
            chunk = plane * PARTS + place
            cut = pl.ds(place * part, part)
            for step in range(1, groups):
                for which in range(REQ):
                    chosen = asked_s[groups - step, 0, which]
                    for way in range(3):
                        out_box[chunk][step - 1, which, way] = own[plane][chosen, way, cut, :]
                far_copy(chunk, step).start()

        for place in range(PARTS):
            chunk = plane * PARTS + place
            cut = pl.ds(place * part, part)
            for step in range(1, groups):
                far_copy(chunk, step).wait_recv()
            if chunk >= 2:
                result_copy(chunk - 2).wait()
            weight = -weight_v[plane, cut, :]

            @pl.loop(0, readings // 4)
            def _(block, plane=plane, chunk=chunk, cut=cut, weight=weight):
                for k in range(4):
                    m = block * 4 + k
                    a, b, c, d = index[4 * m], index[4 * m + 1], index[4 * m + 2], index[4 * m + 3]
                    total = None
                    for way in range(3):
                        first = own[plane][a, way, cut, :].astype(jnp.float32)
                        second = own[plane][b, way, cut, :].astype(jnp.float32)
                        third = far[chunk][c, way].astype(jnp.float32)
                        fourth = far[chunk][d, way].astype(jnp.float32)
                        term = (first - second) * (third - fourth)
                        total = term if total is None else total + term
                    result[chunk % 2][m] = (weight * total).astype(jnp.bfloat16)

            result_copy(chunk).start()

    chunks = planes * PARTS
    for chunk in range(max(chunks - 2, 0), chunks):
        result_copy(chunk).wait()
    for chunk in range(chunks):
        for step in range(1, groups):
            far_copy(chunk, step).wait_send()
    for plane in range(planes):
        for step in range(1, slabs):
            p_copy(plane, step).wait_send()
            gz_copy(plane, step).wait_send()
    for step in range(1, slabs):
        cond_copy(step).wait_send()


def exchange(potentials, conductivity, asked, index, slabs, groups):
    count, depth, rows, width = potentials.shape
    readings = index.shape[0]
    planes = depth // slabs
    x_size = rows * slabs
    part = x_size // PARTS
    hbm = pl.BlockSpec(memory_space=pl.ANY)
    dma = pltpu.SemaphoreType.DMA
    bf16, f32 = jnp.bfloat16, jnp.float32
    chunks = planes * PARTS
    return pl.pallas_call(
        functools.partial(exchange_kernel, slabs, groups, planes),
        out_shape=jax.ShapeDtypeStruct((readings, planes, x_size, width), bf16),
        in_specs=[hbm, hbm, pl.BlockSpec(memory_space=pltpu.VMEM), pl.BlockSpec(memory_space=pltpu.SMEM)],
        out_specs=hbm,
        scratch_shapes=[
            pltpu.VMEM((count, depth, rows, width), f32),
            pltpu.VMEM((planes, slabs, count, rows, width), bf16),
            pltpu.VMEM((groups, 8, 128), jnp.int32),
            pltpu.SMEM((groups, 8, 128), jnp.int32),
            pltpu.VMEM((planes, x_size, width), f32),
        ]
        + [pltpu.VMEM((count, x_size, width), f32)] * planes
        + [pltpu.VMEM((count, 3, x_size, width), bf16)] * planes
        + [pltpu.VMEM(((groups - 1) * REQ, 3, part, width), bf16)] * chunks
        + [pltpu.VMEM((groups - 1, REQ, 3, part, width), bf16)] * chunks
        + [pltpu.VMEM((readings, part, width), bf16)] * 2
        + [
            dma((2, planes, slabs)),
            dma((2, planes, slabs)),
            dma((slabs,)),
            dma((slabs,)),
            dma((groups,)),
            dma((groups,)),
            dma((chunks, groups)),
            dma((chunks, groups)),
            dma((5 + 2 * planes,)),
        ],
        compiler_params=pltpu.CompilerParams(
            collective_id=0, has_side_effects=True, vmem_limit_bytes=61 * 1024 * 1024
        ),
        name="exchange",
    )(potentials, conductivity, asked, index.reshape(-1))


def general(potentials, conductivity, quadrupoles):
    shifted = lax.all_to_all(potentials, "slab", split_axis=1, concat_axis=2, tiled=True)
    cond = lax.all_to_all(conductivity[None], "slab", split_axis=1, concat_axis=2, tiled=True)[0]
    slabs = lax.axis_size("slab")
    ends = slabs - 1
    last = shifted.shape[1] - 1
    below = lax.ppermute(shifted[:, last:], "slab", [(i, i + 1) for i in range(ends)])
    above = lax.ppermute(shifted[:, :1], "slab", [(i + 1, i) for i in range(ends)])
    tall = jnp.concatenate([below, shifted, above], axis=1)
    wide = jnp.pad(shifted, ((0, 0), (0, 0), (1, 1), (1, 1)))
    grads = jnp.stack(
        [
            (tall[:, 2:] - tall[:, :-2]) * 0.5,
            (wide[:, :, 2:, 1:-1] - wide[:, :, :-2, 1:-1]) * 0.5,
            (wide[:, :, 1:-1, 2:] - wide[:, :, 1:-1, :-2]) * 0.5,
        ],
        1,
    ).astype(jnp.bfloat16)
    table = lax.all_gather(grads.reshape(grads.shape[0], 3, -1), "elec", axis=0, tiled=True)
    ids = jnp.arange(table.shape[0], dtype=jnp.int32)
    hot = (quadrupoles[:, :, None] == ids).astype(jnp.bfloat16)
    flat = table.reshape(table.shape[0], -1)
    shape = (quadrupoles.shape[0], 3, -1)
    source = jnp.dot(hot[:, 0] - hot[:, 1], flat, preferred_element_type=jnp.float32).reshape(shape)
    probe = jnp.dot(hot[:, 2] - hot[:, 3], flat, preferred_element_type=jnp.float32).reshape(shape)
    rows = -(cond.reshape(-1)[None] * jnp.sum(source * probe, axis=1))
    return rows.astype(jnp.bfloat16).reshape((quadrupoles.shape[0],) + shifted.shape[1:])


def shards(potentials, conductivity, quadrupoles):
    slabs, groups = lax.axis_size("slab"), lax.axis_size("elec")
    count, depth, rows, width = potentials.shape
    if rows % 16 or width % 128 or depth % slabs or (rows * slabs) % (16 * PARTS) or quadrupoles.shape[0] % 4:
        return general(potentials, conductivity, quadrupoles)
    index, asked = lists(quadrupoles, count, groups)
    return exchange(potentials, conductivity, asked, index, slabs, groups)


def solution(mesh):
    in_specs = (P("elec", None, "slab", None), P(None, "slab", None), P("elec", None))
    out_specs = P("elec", "slab", None, None)
    return jax.shard_map(shards, mesh=mesh, in_specs=in_specs, out_specs=out_specs, check_vma=False)
```

```python
import functools

import jax
import jax.numpy as jnp
from jax import lax
from jax.experimental import pallas as pl
from jax.experimental.pallas import tpu as pltpu
from jax.sharding import PartitionSpec as P

MESH = pl.DeviceIdType.MESH
REQ = 4
PARTS = 4


def lists(quadrupoles, per_group, groups):
    me = lax.axis_index("elec")
    ids = jnp.arange(per_group * groups, dtype=jnp.int32)
    owner = ids // per_group
    away = (owner - me) % groups
    named = jnp.any(quadrupoles[:, 2:4].reshape(-1)[:, None] == ids[None, :], axis=0)
    before = (owner[:, None] == owner[None, :]) & (ids[None, :] < ids[:, None])
    rank = jnp.sum((before & named[None, :]).astype(jnp.int32), axis=1)
    other = (away - 1) * REQ + jnp.minimum(rank, REQ - 1)
    slot = jnp.where(away == 0, ids - me * per_group, other)
    index = jnp.sum(jnp.where(quadrupoles[:, :, None] == ids, slot, 0), axis=-1)
    steps = jnp.arange(groups, dtype=jnp.int32)[:, None, None]
    lanes = jnp.arange(128, dtype=jnp.int32)[None, :, None]
    hit = named & (away == steps) & (rank == lanes)
    asked = jnp.sum(jnp.where(hit, ids % per_group, 0), axis=-1)
    return index.astype(jnp.int32), jnp.broadcast_to(asked[:, None, :], (groups, 8, 128))


def minus(first, second):
    return first.astype(jnp.float32) - second.astype(jnp.float32)


def exchange_kernel(slabs, groups, planes, *refs):
    pot, cond, asked, index, out = refs[:5]
    pot_v, gz_src, asked_in, asked_s, weight_v = refs[5:10]
    p_in = refs[10 : 10 + planes]
    rest = list(refs[10 + planes :])

    def take(n):
        taken = rest[:n]
        del rest[:n]
        return taken

    own_z, own_xy, far_xy, box_xy = take(planes), take(planes), take(planes), take(planes)
    far_z, box_z, result = take(planes * PARTS), take(planes * PARTS), take(2)
    slab_send, slab_recv, cond_send, cond_recv, ask_send, ask_recv, xy_send, xy_recv, far_send, far_recv, local = rest

    count, depth, rows, width = pot.shape
    me = lax.axis_index("slab")
    group = lax.axis_index("elec")
    my_rows = pl.ds(pl.multiple_of(me * rows, rows), rows)

    stage = pltpu.make_async_copy(pot, pot_v, local.at[0])
    stage.start()

    barrier = pltpu.get_barrier_semaphore()
    for step in range(1, slabs):
        pl.semaphore_signal(barrier, inc=1, device_id={"slab": lax.rem(me + step, slabs)}, device_id_type=MESH)
    for step in range(1, groups):
        pl.semaphore_signal(barrier, inc=1, device_id={"elec": lax.rem(group + step, groups)}, device_id_type=MESH)
    pl.semaphore_wait(barrier, slabs + groups - 2)

    asks = []
    for step in range(1, groups):
        copy = pltpu.make_async_remote_copy(
            src_ref=asked.at[step],
            dst_ref=asked_in.at[step],
            send_sem=ask_send.at[step],
            recv_sem=ask_recv.at[step],
            device_id={"elec": lax.rem(group + step, groups)},
            device_id_type=MESH,
        )
        copy.start()
        asks.append(copy)

    def p_copy(plane, step):
        to = lax.rem(me + step, slabs)
        return pltpu.make_async_remote_copy(
            src_ref=pot.at[:, to * planes + plane],
            dst_ref=p_in[plane].at[:, my_rows, :],
            send_sem=slab_send.at[0, plane, step],
            recv_sem=slab_recv.at[0, plane, step],
            device_id={"slab": to},
            device_id_type=MESH,
        )

    def gz_copy(plane, step):
        to = lax.rem(me + step, slabs)
        return pltpu.make_async_remote_copy(
            src_ref=gz_src.at[plane, to],
            dst_ref=own_z[plane].at[:, my_rows, :],
            send_sem=slab_send.at[1, plane, step],
            recv_sem=slab_recv.at[1, plane, step],
            device_id={"slab": to},
            device_id_type=MESH,
        )

    def cond_copy(step):
        to = lax.rem(me + step, slabs)
        return pltpu.make_async_remote_copy(
            src_ref=cond.at[pl.ds(to * planes, planes)],
            dst_ref=weight_v.at[:, my_rows, :],
            send_sem=cond_send.at[step],
            recv_sem=cond_recv.at[step],
            device_id={"slab": to},
            device_id_type=MESH,
        )

    def p_local(plane):
        return pltpu.make_async_copy(pot.at[:, me * planes + plane], p_in[plane].at[:, my_rows, :], local.at[1 + plane])

    def gz_local(plane):
        return pltpu.make_async_copy(
            gz_src.at[plane, me], own_z[plane].at[:, my_rows, :], local.at[1 + planes + plane]
        )

    cond_local = pltpu.make_async_copy(
        cond.at[pl.ds(me * planes, planes)], weight_v.at[:, my_rows, :], local.at[1 + 2 * planes]
    )

    for step in range(1, slabs):
        cond_copy(step).start()
    cond_local.start()
    for plane in range(planes):
        for step in range(1, slabs):
            p_copy(plane, step).start()
        p_local(plane).start()
        if plane == 0:
            stage.wait()

        @pl.loop(0, count)
        def _(e, plane=plane):
            for to in range(slabs):
                z = to * planes + plane
                above = pot_v[e, z + 1] if z + 1 < depth else jnp.zeros((rows, width), jnp.float32)
                below = pot_v[e, z - 1] if z > 0 else jnp.zeros((rows, width), jnp.float32)
                gz_src[plane, to, e] = ((above - below) * 0.5).astype(jnp.bfloat16)

        for step in range(1, slabs):
            gz_copy(plane, step).start()
        gz_local(plane).start()
    for copy in asks:
        copy.wait()
    to_scalar = pltpu.make_async_copy(asked_in, asked_s, local.at[2 + 2 * planes])
    to_scalar.start()
    to_scalar.wait()

    for step in range(1, slabs):
        cond_copy(step).wait_recv()
    cond_local.wait()

    x_size = p_in[0].shape[1]
    part = x_size // PARTS
    readings = out.shape[0]
    row = lax.broadcasted_iota(jnp.int32, (x_size, width), 0)
    lane = lax.broadcasted_iota(jnp.int32, (x_size, width), 1)

    def far_copy(chunk, step):
        return pltpu.make_async_remote_copy(
            src_ref=box_z[chunk].at[step - 1],
            dst_ref=far_z[chunk].at[pl.ds((groups - 1 - step) * REQ, REQ)],
            send_sem=far_send.at[chunk, step],
            recv_sem=far_recv.at[chunk, step],
            device_id={"elec": lax.rem(group + step, groups)},
            device_id_type=MESH,
        )

    def xy_copy(plane, step):
        return pltpu.make_async_remote_copy(
            src_ref=box_xy[plane].at[step - 1],
            dst_ref=far_xy[plane].at[pl.ds((groups - 1 - step) * REQ, REQ)],
            send_sem=xy_send.at[plane, step],
            recv_sem=xy_recv.at[plane, step],
            device_id={"elec": lax.rem(group + step, groups)},
            device_id_type=MESH,
        )

    def result_copy(chunk):
        plane, place = divmod(chunk, PARTS)
        return pltpu.make_async_copy(
            result[chunk % 2], out.at[:, plane, pl.ds(place * part, part), :], local.at[3 + 2 * planes + chunk % 2]
        )

    for plane in range(planes):
        for step in range(1, slabs):
            p_copy(plane, step).wait_recv()
        p_local(plane).wait()

        @pl.loop(0, count)
        def _(e, plane=plane):
            p = p_in[plane][e]
            up = jnp.where(row < x_size - 1, pltpu.roll(p, x_size - 1, 0), 0.0)
            down = jnp.where(row > 0, pltpu.roll(p, 1, 0), 0.0)
            own_xy[plane][e, 0] = ((up - down) * 0.5).astype(jnp.bfloat16)
            right = jnp.where(lane < width - 1, pltpu.roll(p, width - 1, 1), 0.0)
            left = jnp.where(lane > 0, pltpu.roll(p, 1, 1), 0.0)
            own_xy[plane][e, 1] = ((right - left) * 0.5).astype(jnp.bfloat16)

        for step in range(1, groups):
            for which in range(REQ):
                chosen = asked_s[groups - step, 0, which]
                for way in range(2):
                    box_xy[plane][step - 1, which, way] = own_xy[plane][chosen, way]
            xy_copy(plane, step).start()

        for step in range(1, slabs):
            gz_copy(plane, step).wait_recv()
        gz_local(plane).wait()

        for place in range(PARTS):
            chunk = plane * PARTS + place
            cut = pl.ds(place * part, part)
            for step in range(1, groups):
                for which in range(REQ):
                    chosen = asked_s[groups - step, 0, which]
                    box_z[chunk][step - 1, which] = own_z[plane][chosen, cut, :]
                far_copy(chunk, step).start()

        for step in range(1, groups):
            xy_copy(plane, step).wait_recv()
        for place in range(PARTS):
            chunk = plane * PARTS + place
            cut = pl.ds(place * part, part)
            for step in range(1, groups):
                far_copy(chunk, step).wait_recv()
            if chunk >= 2:
                result_copy(chunk - 2).wait()
            weight = -weight_v[plane, cut, :]

            @pl.loop(0, readings // 4)
            def _(block, plane=plane, chunk=chunk, cut=cut, weight=weight):
                for k in range(4):
                    m = block * 4 + k
                    a, b, c, d = index[4 * m], index[4 * m + 1], index[4 * m + 2], index[4 * m + 3]
                    first, second = own_z[plane][a, cut, :], own_z[plane][b, cut, :]
                    third, fourth = far_z[chunk][c], far_z[chunk][d]
                    total = minus(first, second) * minus(third, fourth)
                    for way in range(2):
                        first, second = own_xy[plane][a, way, cut, :], own_xy[plane][b, way, cut, :]
                        third, fourth = far_xy[plane][c, way, cut, :], far_xy[plane][d, way, cut, :]
                        total = total + minus(first, second) * minus(third, fourth)
                    result[chunk % 2][m] = (weight * total).astype(jnp.bfloat16)

            result_copy(chunk).start()

    chunks = planes * PARTS
    for chunk in range(max(chunks - 2, 0), chunks):
        result_copy(chunk).wait()
    for chunk in range(chunks):
        for step in range(1, groups):
            far_copy(chunk, step).wait_send()
    for plane in range(planes):
        for step in range(1, groups):
            xy_copy(plane, step).wait_send()
        for step in range(1, slabs):
            p_copy(plane, step).wait_send()
            gz_copy(plane, step).wait_send()
    for step in range(1, slabs):
        cond_copy(step).wait_send()


def exchange(potentials, conductivity, asked, index, slabs, groups):
    count, depth, rows, width = potentials.shape
    readings = index.shape[0]
    planes = depth // slabs
    x_size = rows * slabs
    part = x_size // PARTS
    hbm = pl.BlockSpec(memory_space=pl.ANY)
    dma = pltpu.SemaphoreType.DMA
    bf16, f32 = jnp.bfloat16, jnp.float32
    chunks = planes * PARTS
    return pl.pallas_call(
        functools.partial(exchange_kernel, slabs, groups, planes),
        out_shape=jax.ShapeDtypeStruct((readings, planes, x_size, width), bf16),
        in_specs=[hbm, hbm, pl.BlockSpec(memory_space=pltpu.VMEM), pl.BlockSpec(memory_space=pltpu.SMEM)],
        out_specs=hbm,
        scratch_shapes=[
            pltpu.VMEM((count, depth, rows, width), f32),
            pltpu.VMEM((planes, slabs, count, rows, width), bf16),
            pltpu.VMEM((groups, 8, 128), jnp.int32),
            pltpu.SMEM((groups, 8, 128), jnp.int32),
            pltpu.VMEM((planes, x_size, width), f32),
        ]
        + [pltpu.VMEM((count, x_size, width), f32)] * planes
        + [pltpu.VMEM((count, x_size, width), bf16)] * planes
        + [pltpu.VMEM((count, 2, x_size, width), bf16)] * planes
        + [pltpu.VMEM(((groups - 1) * REQ, 2, x_size, width), bf16)] * planes
        + [pltpu.VMEM((groups - 1, REQ, 2, x_size, width), bf16)] * planes
        + [pltpu.VMEM(((groups - 1) * REQ, part, width), bf16)] * chunks
        + [pltpu.VMEM((groups - 1, REQ, part, width), bf16)] * chunks
        + [pltpu.VMEM((readings, part, width), bf16)] * 2
        + [
            dma((2, planes, slabs)),
            dma((2, planes, slabs)),
            dma((slabs,)),
            dma((slabs,)),
            dma((groups,)),
            dma((groups,)),
            dma((planes, groups)),
            dma((planes, groups)),
            dma((chunks, groups)),
            dma((chunks, groups)),
            dma((5 + 2 * planes,)),
        ],
        compiler_params=pltpu.CompilerParams(
            collective_id=0, has_side_effects=True, vmem_limit_bytes=29 * 1024 * 1024
        ),
        name="exchange",
    )(potentials, conductivity, asked, index.reshape(-1))


def deliver_kernel(source, target, done):
    share = source.shape[0] // PARTS
    copies = [
        pltpu.make_async_copy(source.at[pl.ds(k * share, share)], target.at[pl.ds(k * share, share)], done.at[k])
        for k in range(PARTS)
    ]
    for copy in copies:
        copy.start()
    for copy in copies:
        copy.wait()


def deliver(rows):
    return pl.pallas_call(
        deliver_kernel,
        out_shape=jax.ShapeDtypeStruct(rows.shape, rows.dtype),
        in_specs=[pl.BlockSpec(memory_space=pl.ANY)],
        out_specs=pl.BlockSpec(memory_space=pl.ANY),
        scratch_shapes=[pltpu.SemaphoreType.DMA((PARTS,))],
        compiler_params=pltpu.CompilerParams(vmem_limit_bytes=1024 * 1024),
        name="deliver",
    )(rows)


def general(potentials, conductivity, quadrupoles):
    shifted = lax.all_to_all(potentials, "slab", split_axis=1, concat_axis=2, tiled=True)
    cond = lax.all_to_all(conductivity[None], "slab", split_axis=1, concat_axis=2, tiled=True)[0]
    slabs = lax.axis_size("slab")
    ends = slabs - 1
    last = shifted.shape[1] - 1
    below = lax.ppermute(shifted[:, last:], "slab", [(i, i + 1) for i in range(ends)])
    above = lax.ppermute(shifted[:, :1], "slab", [(i + 1, i) for i in range(ends)])
    tall = jnp.concatenate([below, shifted, above], axis=1)
    wide = jnp.pad(shifted, ((0, 0), (0, 0), (1, 1), (1, 1)))
    grads = jnp.stack(
        [
            (tall[:, 2:] - tall[:, :-2]) * 0.5,
            (wide[:, :, 2:, 1:-1] - wide[:, :, :-2, 1:-1]) * 0.5,
            (wide[:, :, 1:-1, 2:] - wide[:, :, 1:-1, :-2]) * 0.5,
        ],
        1,
    ).astype(jnp.bfloat16)
    table = lax.all_gather(grads.reshape(grads.shape[0], 3, -1), "elec", axis=0, tiled=True)
    ids = jnp.arange(table.shape[0], dtype=jnp.int32)
    hot = (quadrupoles[:, :, None] == ids).astype(jnp.bfloat16)
    flat = table.reshape(table.shape[0], -1)
    shape = (quadrupoles.shape[0], 3, -1)
    source = jnp.dot(hot[:, 0] - hot[:, 1], flat, preferred_element_type=jnp.float32).reshape(shape)
    probe = jnp.dot(hot[:, 2] - hot[:, 3], flat, preferred_element_type=jnp.float32).reshape(shape)
    rows = -(cond.reshape(-1)[None] * jnp.sum(source * probe, axis=1))
    return rows.astype(jnp.bfloat16).reshape((quadrupoles.shape[0],) + shifted.shape[1:])


def shards(potentials, conductivity, quadrupoles):
    slabs, groups = lax.axis_size("slab"), lax.axis_size("elec")
    count, depth, rows, width = potentials.shape
    if rows % 16 or width % 128 or depth % slabs or (rows * slabs) % (16 * PARTS) or quadrupoles.shape[0] % 4:
        return general(potentials, conductivity, quadrupoles)
    index, asked = lists(quadrupoles, count, groups)
    return deliver(exchange(potentials, conductivity, asked, index, slabs, groups))


def solution(mesh):
    in_specs = (P("elec", None, "slab", None), P(None, "slab", None), P("elec", None))
    out_specs = P("elec", "slab", None, None)
    return jax.shard_map(shards, mesh=mesh, in_specs=in_specs, out_specs=out_specs, check_vma=False)
```

```python
import functools

import jax
import jax.numpy as jnp
from jax import lax
from jax.experimental import pallas as pl
from jax.experimental.pallas import tpu as pltpu
from jax.sharding import PartitionSpec as P

MESH = pl.DeviceIdType.MESH
REQ = 4
PARTS = 4


def lists(quadrupoles, per_group, groups):
    me = lax.axis_index("elec")
    ids = jnp.arange(per_group * groups, dtype=jnp.int32)
    owner = ids // per_group
    away = (owner - me) % groups
    named = jnp.any(quadrupoles[:, 2:4].reshape(-1)[:, None] == ids[None, :], axis=0)
    before = (owner[:, None] == owner[None, :]) & (ids[None, :] < ids[:, None])
    rank = jnp.sum((before & named[None, :]).astype(jnp.int32), axis=1)
    other = (away - 1) * REQ + jnp.minimum(rank, REQ - 1)
    slot = jnp.where(away == 0, ids - me * per_group, other)
    index = jnp.sum(jnp.where(quadrupoles[:, :, None] == ids, slot, 0), axis=-1)
    steps = jnp.arange(groups, dtype=jnp.int32)[:, None, None]
    lanes = jnp.arange(128, dtype=jnp.int32)[None, :, None]
    hit = named & (away == steps) & (rank == lanes)
    asked = jnp.sum(jnp.where(hit, ids % per_group, 0), axis=-1)
    return index.astype(jnp.int32), jnp.broadcast_to(asked[:, None, :], (groups, 8, 128))


def minus(first, second):
    return first.astype(jnp.float32) - second.astype(jnp.float32)


def exchange_kernel(slabs, groups, planes, *refs):
    pot, cond, asked, index, out = refs[:5]
    pot_v, gz_src, asked_in, asked_s, weight_v = refs[5:10]
    p_in = refs[10 : 10 + planes]
    rest = list(refs[10 + planes :])

    def take(n):
        taken = rest[:n]
        del rest[:n]
        return taken

    own_z, own_xy, far_xy, box_xy = take(planes), take(planes), take(planes), take(planes)
    far_z, box_z, result = take(planes * PARTS), take(planes * PARTS), take(2)
    slab_send, slab_recv, cond_send, cond_recv, ask_send, ask_recv, xy_send, xy_recv, far_send, far_recv, local = rest

    count, depth, rows, width = pot.shape
    me = lax.axis_index("slab")
    group = lax.axis_index("elec")
    far_first = sorted(range(1, slabs), key=lambda step: abs(2 * step - slabs))
    my_rows = pl.ds(pl.multiple_of(me * rows, rows), rows)

    stage = pltpu.make_async_copy(pot, pot_v, local.at[0])
    stage.start()

    barrier = pltpu.get_barrier_semaphore()
    for step in range(1, slabs):
        pl.semaphore_signal(barrier, inc=1, device_id={"slab": lax.rem(me + step, slabs)}, device_id_type=MESH)
    for step in range(1, groups):
        pl.semaphore_signal(barrier, inc=1, device_id={"elec": lax.rem(group + step, groups)}, device_id_type=MESH)
    pl.semaphore_wait(barrier, slabs + groups - 2)

    asks = []
    for step in range(1, groups):
        copy = pltpu.make_async_remote_copy(
            src_ref=asked.at[step],
            dst_ref=asked_in.at[step],
            send_sem=ask_send.at[step],
            recv_sem=ask_recv.at[step],
            device_id={"elec": lax.rem(group + step, groups)},
            device_id_type=MESH,
        )
        copy.start()
        asks.append(copy)

    def p_copy(plane, step):
        to = lax.rem(me + step, slabs)
        return pltpu.make_async_remote_copy(
            src_ref=pot.at[:, to * planes + plane],
            dst_ref=p_in[plane].at[:, my_rows, :],
            send_sem=slab_send.at[0, plane, step],
            recv_sem=slab_recv.at[0, plane, step],
            device_id={"slab": to},
            device_id_type=MESH,
        )

    def gz_copy(plane, step):
        to = lax.rem(me + step, slabs)
        return pltpu.make_async_remote_copy(
            src_ref=gz_src.at[plane, to],
            dst_ref=own_z[plane].at[:, my_rows, :],
            send_sem=slab_send.at[1, plane, step],
            recv_sem=slab_recv.at[1, plane, step],
            device_id={"slab": to},
            device_id_type=MESH,
        )

    def cond_copy(step):
        to = lax.rem(me + step, slabs)
        return pltpu.make_async_remote_copy(
            src_ref=cond.at[pl.ds(to * planes, planes)],
            dst_ref=weight_v.at[:, my_rows, :],
            send_sem=cond_send.at[step],
            recv_sem=cond_recv.at[step],
            device_id={"slab": to},
            device_id_type=MESH,
        )

    def p_local(plane):
        return pltpu.make_async_copy(pot.at[:, me * planes + plane], p_in[plane].at[:, my_rows, :], local.at[1 + plane])

    def gz_local(plane):
        return pltpu.make_async_copy(
            gz_src.at[plane, me], own_z[plane].at[:, my_rows, :], local.at[1 + planes + plane]
        )

    cond_local = pltpu.make_async_copy(
        cond.at[pl.ds(me * planes, planes)], weight_v.at[:, my_rows, :], local.at[1 + 2 * planes]
    )

    for step in range(1, slabs):
        cond_copy(step).start()
    cond_local.start()
    for plane in range(planes):
        for step in far_first:
            p_copy(plane, step).start()
        p_local(plane).start()
        if plane == 0:
            stage.wait()

        @pl.loop(0, count)
        def _(e, plane=plane):
            for to in range(slabs):
                z = to * planes + plane
                above = pot_v[e, z + 1] if z + 1 < depth else jnp.zeros((rows, width), jnp.float32)
                below = pot_v[e, z - 1] if z > 0 else jnp.zeros((rows, width), jnp.float32)
                gz_src[plane, to, e] = ((above - below) * 0.5).astype(jnp.bfloat16)

        for step in far_first:
            gz_copy(plane, step).start()
        gz_local(plane).start()
    for copy in asks:
        copy.wait()
    to_scalar = pltpu.make_async_copy(asked_in, asked_s, local.at[2 + 2 * planes])
    to_scalar.start()
    to_scalar.wait()

    for step in range(1, slabs):
        cond_copy(step).wait_recv()
    cond_local.wait()

    x_size = p_in[0].shape[1]
    part = x_size // PARTS
    readings = out.shape[0]
    row = lax.broadcasted_iota(jnp.int32, (x_size, width), 0)
    lane = lax.broadcasted_iota(jnp.int32, (x_size, width), 1)

    def far_copy(chunk, step):
        return pltpu.make_async_remote_copy(
            src_ref=box_z[chunk].at[step - 1],
            dst_ref=far_z[chunk].at[pl.ds((groups - 1 - step) * REQ, REQ)],
            send_sem=far_send.at[chunk, step],
            recv_sem=far_recv.at[chunk, step],
            device_id={"elec": lax.rem(group + step, groups)},
            device_id_type=MESH,
        )

    def xy_copy(plane, step):
        return pltpu.make_async_remote_copy(
            src_ref=box_xy[plane].at[step - 1],
            dst_ref=far_xy[plane].at[pl.ds((groups - 1 - step) * REQ, REQ)],
            send_sem=xy_send.at[plane, step],
            recv_sem=xy_recv.at[plane, step],
            device_id={"elec": lax.rem(group + step, groups)},
            device_id_type=MESH,
        )

    def result_copy(chunk):
        plane, place = divmod(chunk, PARTS)
        return pltpu.make_async_copy(
            result[chunk % 2], out.at[:, plane, pl.ds(place * part, part), :], local.at[3 + 2 * planes + chunk % 2]
        )

    for plane in range(planes):
        for step in range(1, slabs):
            p_copy(plane, step).wait_recv()
        p_local(plane).wait()

        @pl.loop(0, count)
        def _(e, plane=plane):
            p = p_in[plane][e]
            up = jnp.where(row < x_size - 1, pltpu.roll(p, x_size - 1, 0), 0.0)
            down = jnp.where(row > 0, pltpu.roll(p, 1, 0), 0.0)
            own_xy[plane][e, 0] = ((up - down) * 0.5).astype(jnp.bfloat16)
            right = jnp.where(lane < width - 1, pltpu.roll(p, width - 1, 1), 0.0)
            left = jnp.where(lane > 0, pltpu.roll(p, 1, 1), 0.0)
            own_xy[plane][e, 1] = ((right - left) * 0.5).astype(jnp.bfloat16)

        for step in range(1, groups):
            for which in range(REQ):
                chosen = asked_s[groups - step, 0, which]
                for way in range(2):
                    box_xy[plane][step - 1, which, way] = own_xy[plane][chosen, way]
            xy_copy(plane, step).start()

        for step in range(1, slabs):
            gz_copy(plane, step).wait_recv()
        gz_local(plane).wait()

        for place in range(PARTS):
            chunk = plane * PARTS + place
            cut = pl.ds(place * part, part)
            for step in range(1, groups):
                for which in range(REQ):
                    chosen = asked_s[groups - step, 0, which]
                    box_z[chunk][step - 1, which] = own_z[plane][chosen, cut, :]
                far_copy(chunk, step).start()

        for step in range(1, groups):
            xy_copy(plane, step).wait_recv()
        for place in range(PARTS):
            chunk = plane * PARTS + place
            cut = pl.ds(place * part, part)
            for step in range(1, groups):
                far_copy(chunk, step).wait_recv()
            if chunk >= 2:
                result_copy(chunk - 2).wait()
            weight = -weight_v[plane, cut, :]

            @pl.loop(0, readings // 4)
            def _(block, plane=plane, chunk=chunk, cut=cut, weight=weight):
                for k in range(4):
                    m = block * 4 + k
                    a, b, c, d = index[4 * m], index[4 * m + 1], index[4 * m + 2], index[4 * m + 3]
                    first, second = own_z[plane][a, cut, :], own_z[plane][b, cut, :]
                    third, fourth = far_z[chunk][c], far_z[chunk][d]
                    total = minus(first, second) * minus(third, fourth)
                    for way in range(2):
                        first, second = own_xy[plane][a, way, cut, :], own_xy[plane][b, way, cut, :]
                        third, fourth = far_xy[plane][c, way, cut, :], far_xy[plane][d, way, cut, :]
                        total = total + minus(first, second) * minus(third, fourth)
                    result[chunk % 2][m] = (weight * total).astype(jnp.bfloat16)

            result_copy(chunk).start()

    chunks = planes * PARTS
    for chunk in range(max(chunks - 2, 0), chunks):
        result_copy(chunk).wait()
    for chunk in range(chunks):
        for step in range(1, groups):
            far_copy(chunk, step).wait_send()
    for plane in range(planes):
        for step in range(1, groups):
            xy_copy(plane, step).wait_send()
        for step in range(1, slabs):
            p_copy(plane, step).wait_send()
            gz_copy(plane, step).wait_send()
    for step in range(1, slabs):
        cond_copy(step).wait_send()


def exchange(potentials, conductivity, asked, index, slabs, groups):
    count, depth, rows, width = potentials.shape
    readings = index.shape[0]
    planes = depth // slabs
    x_size = rows * slabs
    part = x_size // PARTS
    hbm = pl.BlockSpec(memory_space=pl.ANY)
    dma = pltpu.SemaphoreType.DMA
    bf16, f32 = jnp.bfloat16, jnp.float32
    chunks = planes * PARTS
    return pl.pallas_call(
        functools.partial(exchange_kernel, slabs, groups, planes),
        out_shape=jax.ShapeDtypeStruct((readings, planes, x_size, width), bf16),
        in_specs=[hbm, hbm, pl.BlockSpec(memory_space=pltpu.VMEM), pl.BlockSpec(memory_space=pltpu.SMEM)],
        out_specs=hbm,
        scratch_shapes=[
            pltpu.VMEM((count, depth, rows, width), f32),
            pltpu.VMEM((planes, slabs, count, rows, width), bf16),
            pltpu.VMEM((groups, 8, 128), jnp.int32),
            pltpu.SMEM((groups, 8, 128), jnp.int32),
            pltpu.VMEM((planes, x_size, width), f32),
        ]
        + [pltpu.VMEM((count, x_size, width), f32)] * planes
        + [pltpu.VMEM((count, x_size, width), bf16)] * planes
        + [pltpu.VMEM((count, 2, x_size, width), bf16)] * planes
        + [pltpu.VMEM(((groups - 1) * REQ, 2, x_size, width), bf16)] * planes
        + [pltpu.VMEM((groups - 1, REQ, 2, x_size, width), bf16)] * planes
        + [pltpu.VMEM(((groups - 1) * REQ, part, width), bf16)] * chunks
        + [pltpu.VMEM((groups - 1, REQ, part, width), bf16)] * chunks
        + [pltpu.VMEM((readings, part, width), bf16)] * 2
        + [
            dma((2, planes, slabs)),
            dma((2, planes, slabs)),
            dma((slabs,)),
            dma((slabs,)),
            dma((groups,)),
            dma((groups,)),
            dma((planes, groups)),
            dma((planes, groups)),
            dma((chunks, groups)),
            dma((chunks, groups)),
            dma((5 + 2 * planes,)),
        ],
        compiler_params=pltpu.CompilerParams(
            collective_id=0, has_side_effects=True, vmem_limit_bytes=29 * 1024 * 1024
        ),
        name="exchange",
    )(potentials, conductivity, asked, index.reshape(-1))


def deliver_kernel(source, target, done):
    share = source.shape[0] // PARTS
    copies = [
        pltpu.make_async_copy(source.at[pl.ds(k * share, share)], target.at[pl.ds(k * share, share)], done.at[k])
        for k in range(PARTS)
    ]
    for copy in copies:
        copy.start()
    for copy in copies:
        copy.wait()


def deliver(rows):
    return pl.pallas_call(
        deliver_kernel,
        out_shape=jax.ShapeDtypeStruct(rows.shape, rows.dtype),
        in_specs=[pl.BlockSpec(memory_space=pl.ANY)],
        out_specs=pl.BlockSpec(memory_space=pl.ANY),
        scratch_shapes=[pltpu.SemaphoreType.DMA((PARTS,))],
        compiler_params=pltpu.CompilerParams(vmem_limit_bytes=1024 * 1024),
        name="deliver",
    )(rows)


def general(potentials, conductivity, quadrupoles):
    shifted = lax.all_to_all(potentials, "slab", split_axis=1, concat_axis=2, tiled=True)
    cond = lax.all_to_all(conductivity[None], "slab", split_axis=1, concat_axis=2, tiled=True)[0]
    slabs = lax.axis_size("slab")
    ends = slabs - 1
    last = shifted.shape[1] - 1
    below = lax.ppermute(shifted[:, last:], "slab", [(i, i + 1) for i in range(ends)])
    above = lax.ppermute(shifted[:, :1], "slab", [(i + 1, i) for i in range(ends)])
    tall = jnp.concatenate([below, shifted, above], axis=1)
    wide = jnp.pad(shifted, ((0, 0), (0, 0), (1, 1), (1, 1)))
    grads = jnp.stack(
        [
            (tall[:, 2:] - tall[:, :-2]) * 0.5,
            (wide[:, :, 2:, 1:-1] - wide[:, :, :-2, 1:-1]) * 0.5,
            (wide[:, :, 1:-1, 2:] - wide[:, :, 1:-1, :-2]) * 0.5,
        ],
        1,
    ).astype(jnp.bfloat16)
    table = lax.all_gather(grads.reshape(grads.shape[0], 3, -1), "elec", axis=0, tiled=True)
    ids = jnp.arange(table.shape[0], dtype=jnp.int32)
    hot = (quadrupoles[:, :, None] == ids).astype(jnp.bfloat16)
    flat = table.reshape(table.shape[0], -1)
    shape = (quadrupoles.shape[0], 3, -1)
    source = jnp.dot(hot[:, 0] - hot[:, 1], flat, preferred_element_type=jnp.float32).reshape(shape)
    probe = jnp.dot(hot[:, 2] - hot[:, 3], flat, preferred_element_type=jnp.float32).reshape(shape)
    rows = -(cond.reshape(-1)[None] * jnp.sum(source * probe, axis=1))
    return rows.astype(jnp.bfloat16).reshape((quadrupoles.shape[0],) + shifted.shape[1:])


def shards(potentials, conductivity, quadrupoles):
    slabs, groups = lax.axis_size("slab"), lax.axis_size("elec")
    count, depth, rows, width = potentials.shape
    if rows % 16 or width % 128 or depth % slabs or (rows * slabs) % (16 * PARTS) or quadrupoles.shape[0] % 4:
        return general(potentials, conductivity, quadrupoles)
    index, asked = lists(quadrupoles, count, groups)
    return deliver(exchange(potentials, conductivity, asked, index, slabs, groups))


def solution(mesh):
    in_specs = (P("elec", None, "slab", None), P(None, "slab", None), P("elec", None))
    out_specs = P("elec", "slab", None, None)
    return jax.shard_map(shards, mesh=mesh, in_specs=in_specs, out_specs=out_specs, check_vma=False)
```

```python
import functools

import jax
import jax.numpy as jnp
from jax import lax
from jax.experimental import pallas as pl
from jax.experimental.pallas import tpu as pltpu
from jax.sharding import PartitionSpec as P

MESH = pl.DeviceIdType.MESH
REQ = 4
PARTS = 4


def lists(quadrupoles, per_group, groups):
    me = lax.axis_index("elec")
    ids = jnp.arange(per_group * groups, dtype=jnp.int32)
    owner = ids // per_group
    away = (owner - me) % groups
    named = jnp.any(quadrupoles[:, 2:4].reshape(-1)[:, None] == ids[None, :], axis=0)
    before = (owner[:, None] == owner[None, :]) & (ids[None, :] < ids[:, None])
    rank = jnp.sum((before & named[None, :]).astype(jnp.int32), axis=1)
    other = (away - 1) * REQ + jnp.minimum(rank, REQ - 1)
    slot = jnp.where(away == 0, ids - me * per_group, other)
    index = jnp.sum(jnp.where(quadrupoles[:, :, None] == ids, slot, 0), axis=-1)
    steps = jnp.arange(groups, dtype=jnp.int32)[:, None, None]
    lanes = jnp.arange(128, dtype=jnp.int32)[None, :, None]
    hit = named & (away == steps) & (rank == lanes)
    asked = jnp.sum(jnp.where(hit, ids % per_group, 0), axis=-1)
    return index.astype(jnp.int32), jnp.broadcast_to(asked[:, None, :], (groups, 8, 128))


def minus(first, second):
    return first.astype(jnp.float32) - second.astype(jnp.float32)


def exchange_kernel(slabs, groups, planes, *refs):
    pot, cond, asked, index, out = refs[:5]
    gz_src, asked_in, asked_s, weight_v = refs[5:9]
    p_in = refs[9 : 9 + planes]
    rest = list(refs[9 + planes :])

    def take(n):
        taken = rest[:n]
        del rest[:n]
        return taken

    own_z, own_xy, far_xy, box_xy = take(planes), take(planes), take(planes), take(planes)
    far_z, box_z, result = take(planes * PARTS), take(planes * PARTS), take(2)
    slab_send, slab_recv, cond_send, cond_recv, ask_send, ask_recv, xy_send, xy_recv, far_send, far_recv, local = rest

    count, depth, rows, width = pot.shape
    me = lax.axis_index("slab")
    group = lax.axis_index("elec")
    my_rows = pl.ds(pl.multiple_of(me * rows, rows), rows)

    barrier = pltpu.get_barrier_semaphore()
    for step in range(1, slabs):
        pl.semaphore_signal(barrier, inc=1, device_id={"slab": lax.rem(me + step, slabs)}, device_id_type=MESH)
    for step in range(1, groups):
        pl.semaphore_signal(barrier, inc=1, device_id={"elec": lax.rem(group + step, groups)}, device_id_type=MESH)
    pl.semaphore_wait(barrier, slabs + groups - 2)

    asks = []
    for step in range(1, groups):
        copy = pltpu.make_async_remote_copy(
            src_ref=asked.at[step],
            dst_ref=asked_in.at[step],
            send_sem=ask_send.at[step],
            recv_sem=ask_recv.at[step],
            device_id={"elec": lax.rem(group + step, groups)},
            device_id_type=MESH,
        )
        copy.start()
        asks.append(copy)

    def p_copy(plane, step):
        to = lax.rem(me + step, slabs)
        return pltpu.make_async_remote_copy(
            src_ref=pot.at[:, to * planes + plane],
            dst_ref=p_in[plane].at[:, my_rows, :],
            send_sem=slab_send.at[0, plane, step],
            recv_sem=slab_recv.at[0, plane, step],
            device_id={"slab": to},
            device_id_type=MESH,
        )

    def gz_copy(plane, step):
        to = lax.rem(me + step, slabs)
        return pltpu.make_async_remote_copy(
            src_ref=gz_src.at[plane, to],
            dst_ref=own_z[plane].at[:, my_rows, :],
            send_sem=slab_send.at[1, plane, step],
            recv_sem=slab_recv.at[1, plane, step],
            device_id={"slab": to},
            device_id_type=MESH,
        )

    def cond_copy(step):
        to = lax.rem(me + step, slabs)
        return pltpu.make_async_remote_copy(
            src_ref=cond.at[pl.ds(to * planes, planes)],
            dst_ref=weight_v.at[:, my_rows, :],
            send_sem=cond_send.at[step],
            recv_sem=cond_recv.at[step],
            device_id={"slab": to},
            device_id_type=MESH,
        )

    def p_local(plane):
        return pltpu.make_async_copy(pot.at[:, me * planes + plane], p_in[plane].at[:, my_rows, :], local.at[1 + plane])

    def gz_local(plane):
        return pltpu.make_async_copy(
            gz_src.at[plane, me], own_z[plane].at[:, my_rows, :], local.at[1 + planes + plane]
        )

    cond_local = pltpu.make_async_copy(
        cond.at[pl.ds(me * planes, planes)], weight_v.at[:, my_rows, :], local.at[1 + 2 * planes]
    )

    for step in range(1, slabs):
        cond_copy(step).start()
    cond_local.start()
    for plane in range(planes):
        for step in range(1, slabs):
            p_copy(plane, step).start()
        p_local(plane).start()

        @pl.loop(0, count)
        def _(e, plane=plane):
            for to in range(slabs):
                z = to * planes + plane
                above = pot[e, z + 1] if z + 1 < depth else jnp.zeros((rows, width), jnp.float32)
                below = pot[e, z - 1] if z > 0 else jnp.zeros((rows, width), jnp.float32)
                gz_src[plane, to, e] = ((above - below) * 0.5).astype(jnp.bfloat16)

        for step in range(1, slabs):
            gz_copy(plane, step).start()
        gz_local(plane).start()
    for copy in asks:
        copy.wait()
    to_scalar = pltpu.make_async_copy(asked_in, asked_s, local.at[2 + 2 * planes])
    to_scalar.start()
    to_scalar.wait()

    for step in range(1, slabs):
        cond_copy(step).wait_recv()
    cond_local.wait()

    x_size = p_in[0].shape[1]
    part = x_size // PARTS
    readings = out.shape[0]
    row = lax.broadcasted_iota(jnp.int32, (x_size, width), 0)
    lane = lax.broadcasted_iota(jnp.int32, (x_size, width), 1)

    def far_copy(chunk, step):
        return pltpu.make_async_remote_copy(
            src_ref=box_z[chunk].at[step - 1],
            dst_ref=far_z[chunk].at[pl.ds((groups - 1 - step) * REQ, REQ)],
            send_sem=far_send.at[chunk, step],
            recv_sem=far_recv.at[chunk, step],
            device_id={"elec": lax.rem(group + step, groups)},
            device_id_type=MESH,
        )

    def xy_copy(plane, step):
        return pltpu.make_async_remote_copy(
            src_ref=box_xy[plane].at[step - 1],
            dst_ref=far_xy[plane].at[pl.ds((groups - 1 - step) * REQ, REQ)],
            send_sem=xy_send.at[plane, step],
            recv_sem=xy_recv.at[plane, step],
            device_id={"elec": lax.rem(group + step, groups)},
            device_id_type=MESH,
        )

    def result_copy(chunk):
        plane, place = divmod(chunk, PARTS)
        return pltpu.make_async_copy(
            result[chunk % 2], out.at[:, plane, pl.ds(place * part, part), :], local.at[3 + 2 * planes + chunk % 2]
        )

    for plane in range(planes):
        for step in range(1, slabs):
            p_copy(plane, step).wait_recv()
        p_local(plane).wait()

        @pl.loop(0, count)
        def _(e, plane=plane):
            p = p_in[plane][e]
            up = jnp.where(row < x_size - 1, pltpu.roll(p, x_size - 1, 0), 0.0)
            down = jnp.where(row > 0, pltpu.roll(p, 1, 0), 0.0)
            own_xy[plane][e, 0] = ((up - down) * 0.5).astype(jnp.bfloat16)
            right = jnp.where(lane < width - 1, pltpu.roll(p, width - 1, 1), 0.0)
            left = jnp.where(lane > 0, pltpu.roll(p, 1, 1), 0.0)
            own_xy[plane][e, 1] = ((right - left) * 0.5).astype(jnp.bfloat16)

        for step in range(1, groups):
            for which in range(REQ):
                chosen = asked_s[groups - step, 0, which]
                for way in range(2):
                    box_xy[plane][step - 1, which, way] = own_xy[plane][chosen, way]
            xy_copy(plane, step).start()

        for step in range(1, slabs):
            gz_copy(plane, step).wait_recv()
        gz_local(plane).wait()

        for place in range(PARTS):
            chunk = plane * PARTS + place
            cut = pl.ds(place * part, part)
            for step in range(1, groups):
                for which in range(REQ):
                    chosen = asked_s[groups - step, 0, which]
                    box_z[chunk][step - 1, which] = own_z[plane][chosen, cut, :]
                far_copy(chunk, step).start()

        for step in range(1, groups):
            xy_copy(plane, step).wait_recv()
        for place in range(PARTS):
            chunk = plane * PARTS + place
            cut = pl.ds(place * part, part)
            for step in range(1, groups):
                far_copy(chunk, step).wait_recv()
            if chunk >= 2:
                result_copy(chunk - 2).wait()
            weight = -weight_v[plane, cut, :]

            @pl.loop(0, readings // 4)
            def _(block, plane=plane, chunk=chunk, cut=cut, weight=weight):
                for k in range(4):
                    m = block * 4 + k
                    a, b, c, d = index[4 * m], index[4 * m + 1], index[4 * m + 2], index[4 * m + 3]
                    first, second = own_z[plane][a, cut, :], own_z[plane][b, cut, :]
                    third, fourth = far_z[chunk][c], far_z[chunk][d]
                    total = minus(first, second) * minus(third, fourth)
                    for way in range(2):
                        first, second = own_xy[plane][a, way, cut, :], own_xy[plane][b, way, cut, :]
                        third, fourth = far_xy[plane][c, way, cut, :], far_xy[plane][d, way, cut, :]
                        total = total + minus(first, second) * minus(third, fourth)
                    result[chunk % 2][m] = (weight * total).astype(jnp.bfloat16)

            result_copy(chunk).start()

    chunks = planes * PARTS
    for chunk in range(max(chunks - 2, 0), chunks):
        result_copy(chunk).wait()
    for chunk in range(chunks):
        for step in range(1, groups):
            far_copy(chunk, step).wait_send()
    for plane in range(planes):
        for step in range(1, groups):
            xy_copy(plane, step).wait_send()
        for step in range(1, slabs):
            p_copy(plane, step).wait_send()
            gz_copy(plane, step).wait_send()
    for step in range(1, slabs):
        cond_copy(step).wait_send()


def exchange(potentials, conductivity, asked, index, slabs, groups):
    count, depth, rows, width = potentials.shape
    readings = index.shape[0]
    planes = depth // slabs
    x_size = rows * slabs
    part = x_size // PARTS
    hbm = pl.BlockSpec(memory_space=pl.ANY)
    dma = pltpu.SemaphoreType.DMA
    bf16, f32 = jnp.bfloat16, jnp.float32
    chunks = planes * PARTS
    return pl.pallas_call(
        functools.partial(exchange_kernel, slabs, groups, planes),
        out_shape=jax.ShapeDtypeStruct((readings, planes, x_size, width), bf16),
        in_specs=[pl.BlockSpec(memory_space=pltpu.VMEM), hbm, pl.BlockSpec(memory_space=pltpu.VMEM), pl.BlockSpec(memory_space=pltpu.SMEM)],
        out_specs=hbm,
        scratch_shapes=[
            pltpu.VMEM((planes, slabs, count, rows, width), bf16),
            pltpu.VMEM((groups, 8, 128), jnp.int32),
            pltpu.SMEM((groups, 8, 128), jnp.int32),
            pltpu.VMEM((planes, x_size, width), f32),
        ]
        + [pltpu.VMEM((count, x_size, width), f32)] * planes
        + [pltpu.VMEM((count, x_size, width), bf16)] * planes
        + [pltpu.VMEM((count, 2, x_size, width), bf16)] * planes
        + [pltpu.VMEM(((groups - 1) * REQ, 2, x_size, width), bf16)] * planes
        + [pltpu.VMEM((groups - 1, REQ, 2, x_size, width), bf16)] * planes
        + [pltpu.VMEM(((groups - 1) * REQ, part, width), bf16)] * chunks
        + [pltpu.VMEM((groups - 1, REQ, part, width), bf16)] * chunks
        + [pltpu.VMEM((readings, part, width), bf16)] * 2
        + [
            dma((2, planes, slabs)),
            dma((2, planes, slabs)),
            dma((slabs,)),
            dma((slabs,)),
            dma((groups,)),
            dma((groups,)),
            dma((planes, groups)),
            dma((planes, groups)),
            dma((chunks, groups)),
            dma((chunks, groups)),
            dma((5 + 2 * planes,)),
        ],
        compiler_params=pltpu.CompilerParams(
            collective_id=0, has_side_effects=True, vmem_limit_bytes=29 * 1024 * 1024
        ),
        name="exchange",
    )(potentials, conductivity, asked, index.reshape(-1))


def deliver_kernel(source, target, done):
    share = source.shape[0] // PARTS
    copies = [
        pltpu.make_async_copy(source.at[pl.ds(k * share, share)], target.at[pl.ds(k * share, share)], done.at[k])
        for k in range(PARTS)
    ]
    for copy in copies:
        copy.start()
    for copy in copies:
        copy.wait()


def deliver(rows):
    return pl.pallas_call(
        deliver_kernel,
        out_shape=jax.ShapeDtypeStruct(rows.shape, rows.dtype),
        in_specs=[pl.BlockSpec(memory_space=pl.ANY)],
        out_specs=pl.BlockSpec(memory_space=pl.ANY),
        scratch_shapes=[pltpu.SemaphoreType.DMA((PARTS,))],
        compiler_params=pltpu.CompilerParams(vmem_limit_bytes=1024 * 1024),
        name="deliver",
    )(rows)


def general(potentials, conductivity, quadrupoles):
    shifted = lax.all_to_all(potentials, "slab", split_axis=1, concat_axis=2, tiled=True)
    cond = lax.all_to_all(conductivity[None], "slab", split_axis=1, concat_axis=2, tiled=True)[0]
    slabs = lax.axis_size("slab")
    ends = slabs - 1
    last = shifted.shape[1] - 1
    below = lax.ppermute(shifted[:, last:], "slab", [(i, i + 1) for i in range(ends)])
    above = lax.ppermute(shifted[:, :1], "slab", [(i + 1, i) for i in range(ends)])
    tall = jnp.concatenate([below, shifted, above], axis=1)
    wide = jnp.pad(shifted, ((0, 0), (0, 0), (1, 1), (1, 1)))
    grads = jnp.stack(
        [
            (tall[:, 2:] - tall[:, :-2]) * 0.5,
            (wide[:, :, 2:, 1:-1] - wide[:, :, :-2, 1:-1]) * 0.5,
            (wide[:, :, 1:-1, 2:] - wide[:, :, 1:-1, :-2]) * 0.5,
        ],
        1,
    ).astype(jnp.bfloat16)
    table = lax.all_gather(grads.reshape(grads.shape[0], 3, -1), "elec", axis=0, tiled=True)
    ids = jnp.arange(table.shape[0], dtype=jnp.int32)
    hot = (quadrupoles[:, :, None] == ids).astype(jnp.bfloat16)
    flat = table.reshape(table.shape[0], -1)
    shape = (quadrupoles.shape[0], 3, -1)
    source = jnp.dot(hot[:, 0] - hot[:, 1], flat, preferred_element_type=jnp.float32).reshape(shape)
    probe = jnp.dot(hot[:, 2] - hot[:, 3], flat, preferred_element_type=jnp.float32).reshape(shape)
    rows = -(cond.reshape(-1)[None] * jnp.sum(source * probe, axis=1))
    return rows.astype(jnp.bfloat16).reshape((quadrupoles.shape[0],) + shifted.shape[1:])


def shards(potentials, conductivity, quadrupoles):
    slabs, groups = lax.axis_size("slab"), lax.axis_size("elec")
    count, depth, rows, width = potentials.shape
    if rows % 16 or width % 128 or depth % slabs or (rows * slabs) % (16 * PARTS) or quadrupoles.shape[0] % 4:
        return general(potentials, conductivity, quadrupoles)
    index, asked = lists(quadrupoles, count, groups)
    return deliver(exchange(potentials, conductivity, asked, index, slabs, groups))


def solution(mesh):
    in_specs = (P("elec", None, "slab", None), P(None, "slab", None), P("elec", None))
    out_specs = P("elec", "slab", None, None)
    return jax.shard_map(shards, mesh=mesh, in_specs=in_specs, out_specs=out_specs, check_vma=False)
```
